32 devices in a mesh: leaf: 4 (over y, core), front: 8 (over z, x).
Axes of the slice: x: 2, y: 2, z: 4, core: 2. Of those that a mesh axis runs over, the one named last changes fastest.
Arguments:
- child_fronts: float32 [4, 4096, 4, 8, 128], P('leaf', None, None, 'front'), as said below
- parent_front: float32 [16, 4, 128, 8, 8, 128], P(None, 'leaf', None, None, 'front'), as said below
- child_map: int32 [4, 24], replicated, may hold values from 0 to 63, as said below
Outputs:
- child_result: float32 [4, 4096, 4, 8, 128], P('leaf', None, None, 'front')
- parent_result: float32 [16, 4, 128, 8, 8, 128], P(None, 'leaf', None, None, 'front')
The draws below stay inside these ranges and needn't reach their ends.
Inputs may be any that keep to these rules, and one draw needn't show every extreme that they name: Row g gives, for each update block v of child g, the parent block that receives it. The entries of a row are distinct, child_map[g, v] mod 8 equals (8 + v) mod 8, and every child's last update block goes to the parent's last block. `child_fronts`: each front is symmetric positive definite. `parent_front`: the parent front is symmetric positive definite.
All inputs are finite; a program needn't handle non-finite values.
Results may differ from the reference program's by a relative error of at most 0.000059.
Values sent between devices are 32-bit elements; how exact they have to be, the bound alone decides.
A program may use at most 256 MiB of HBM per device.

```python
import jax
import jax.numpy as jnp
from jax import lax

BLK = 128
CHILD_ORDER = 4096
CHILD_PIVOTS = 8
PARENT_ORDER = 8192
PARENT_PIVOTS = 2
GROUPS = 4
UPDATE_BLOCKS = 24
CHILD_SLOTS = 4
PARENT_RSLOTS = 16
PARENT_CSLOTS = 8


def symmetric_front(key, order):
    key_raw = jax.random.fold_in(key, 0)
    raw = jax.random.normal(key_raw, (order, order), jnp.float32)
    gram = jnp.dot(raw, raw.T, precision=lax.Precision.HIGHEST) * (1.0 / order)
    gram = 0.5 * (gram + gram.T)
    positions = jnp.arange(order, dtype=jnp.int32)
    shifted = gram + jnp.where(positions[:, None] == positions[None, :], 0.15, 0.0).astype(jnp.float32)
    return shifted


def draw_child_fronts(key, part):
    keys = jax.random.split(jax.random.fold_in(key, 11), GROUPS)
    fronts = lax.map(lambda single: symmetric_front(single, CHILD_ORDER), keys)
    return fronts.reshape(GROUPS, CHILD_ORDER, CHILD_SLOTS, -1, BLK)


def draw_parent_front(key, part):
    matrix = symmetric_front(jax.random.fold_in(key, 23), PARENT_ORDER)
    leaf_count = PARENT_ORDER // BLK // PARENT_RSLOTS
    front_count = PARENT_ORDER // BLK // PARENT_CSLOTS
    return matrix.reshape(PARENT_RSLOTS, leaf_count, BLK, PARENT_CSLOTS, front_count, BLK)


def draw_child_map(key, part):
    front_count = PARENT_ORDER // BLK // PARENT_CSLOTS
    positions = CHILD_PIVOTS + jnp.arange(UPDATE_BLOCKS, dtype=jnp.int32)
    residues = positions % front_count
    ranks = positions // front_count
    last_rank = (CHILD_PIVOTS + UPDATE_BLOCKS - 1) // front_count
    scores = jax.random.randint(jax.random.fold_in(key, 37), (GROUPS, front_count, PARENT_CSLOTS), 0, 1 << 20)
    scores = scores * PARENT_CSLOTS + jnp.arange(PARENT_CSLOTS, dtype=jnp.int32)[None, None, :]
    top_slot = (jnp.arange(front_count, dtype=jnp.int32)[:, None] == front_count - 1) & (jnp.arange(PARENT_CSLOTS, dtype=jnp.int32)[None, :] == PARENT_CSLOTS - 1)
    scores = jnp.where(top_slot[None, :, :], -1, scores)
    orders = jnp.argsort(scores, axis=-1, stable=True).astype(jnp.int32)
    picks = (ranks - last_rank) % PARENT_CSLOTS
    chosen = orders[:, residues, picks]
    return (residues[None, :] + front_count * chosen).astype(jnp.int32)


def setup_inputs(seed: int = 0) -> dict:
    arg_keys = jax.random.split(jax.random.key(seed), 4)
    return {
        "child_fronts": draw_child_fronts(jax.random.fold_in(arg_keys[3], 71), 0),
        "parent_front": draw_parent_front(jax.random.fold_in(arg_keys[3], 71), 0),
        "child_map": draw_child_map(jax.random.fold_in(arg_keys[3], 71), 0),
    }


def partial_factor(front, pivots):
    order = front.shape[0]
    factor = jnp.linalg.cholesky(front[:pivots, :pivots])
    lower_part = jax.scipy.linalg.solve_triangular(factor, front[pivots:, :pivots].T, lower=True).T
    schur = front[pivots:, pivots:] - jnp.dot(lower_part, lower_part.T, precision=lax.Precision.HIGHEST)
    upper = jnp.concatenate([factor, jnp.zeros((pivots, order - pivots), front.dtype)], 1)
    bottom = jnp.concatenate([lower_part, schur], 1)
    return jnp.concatenate([upper, bottom], 0)

def reference(child_fronts, parent_front, child_map):
    groups = child_fronts.shape[0]
    fronts = child_fronts.reshape(groups, CHILD_ORDER, CHILD_ORDER)
    pivot_rows = CHILD_PIVOTS * BLK
    results = lax.map(lambda single: partial_factor(single, pivot_rows), fronts)
    parent = parent_front.reshape(PARENT_ORDER, PARENT_ORDER)
    offsets = jnp.arange(BLK, dtype=jnp.int32)
    for group in range(groups):
        targets = (child_map[group].astype(jnp.int32)[:, None] * BLK + offsets[None, :]).reshape(-1)
        parent = parent.at[targets[:, None], targets[None, :]].add(results[group, pivot_rows:, pivot_rows:])
    parent = partial_factor(parent, PARENT_PIVOTS * BLK)
    return (results.reshape(child_fronts.shape), parent.reshape(parent_front.shape))
```

```python
import jax
import jax.numpy as jnp
from jax import lax
from jax.sharding import PartitionSpec as P

CHILD_PIVOTS = 8
PARENT_PIVOTS = 2
HIGH = lax.Precision.HIGH
HIGHEST = lax.Precision.HIGHEST


def factor_block(square):
    return lax.linalg.cholesky(square, symmetrize_input=False)


def solve_left(factor, rows):
    return lax.linalg.triangular_solve(factor, rows, left_side=True, lower=True)


def factor_strips(work, pivots, block):
    strips = []
    for i in range(pivots):
        start = i * block
        current = work[start : start + block, start:]
        if strips:
            done = jnp.concatenate(
                [strip[:, (i - j) * block :] for j, strip in enumerate(strips)], 0
            )
            current = current - lax.dot_general(
                done[:, :block], done, (((0,), (0,)), ((), ())), precision=HIGHEST
            )
        factor = factor_block(current[:, :block])
        rest = solve_left(factor, current[:, block:])
        strips.append(jnp.concatenate([factor.T, rest], 1))
    return strips


def body(child_fronts, parent_front, child_map):
    front_count = lax.axis_size("front")
    leaf_count = lax.axis_size("leaf")
    front_pos = lax.axis_index("front")
    leaf_pos = lax.axis_index("leaf")
    block = child_fronts.shape[4]
    order = child_fronts.shape[1]
    slots = child_fronts.shape[2]
    pivots = CHILD_PIVOTS
    width = pivots * block
    first_slot = pivots // front_count
    kept = slots - first_slot
    panel_slots = (pivots + front_count - 1) // front_count
    update_count = order // block - pivots
    matrix = child_fronts.reshape(order, slots * block)

    lead = lax.all_gather(matrix[:width, : panel_slots * block], "front", axis=0)
    lead = lead.reshape(front_count, width, panel_slots, block).transpose(1, 2, 0, 3)
    lead = lead.reshape(width, panel_slots * front_count * block)[:, :width]

    own_top = matrix[:width, first_slot * block :]
    strips = factor_strips(jnp.concatenate([lead, own_top], 1), pivots, block)
    gathered = []
    own = []
    lead_columns = []
    for i, strip in enumerate(strips):
        split = width - i * block
        own.append(strip[:, split:])
        gathered.append(
            lax.all_gather(strip[:, split:].T, "front", axis=0, tiled=True).reshape(
                front_count, kept, block, block
            )
        )
        column = strip[:, :split].T
        lead_columns.append(
            jnp.concatenate([jnp.zeros((i * block, block), jnp.float32), column], 0)
        )
    own = jnp.concatenate(own, 0)
    lower = jnp.concatenate(gathered, 3).transpose(1, 0, 2, 3)
    lower = lower.reshape(kept * front_count * block, width)
    lower = lower[width - first_slot * front_count * block :]

    parts = kept if update_count % (kept * leaf_count) == 0 else 1
    part_rows = update_count * block // parts
    sums = []
    received = []
    for part in range(parts):
        low = part * part_rows
        product = lax.dot_general(
            lower[low : low + part_rows], own, (((1,), (0,)), ((), ())), precision=HIGH
        )
        piece = matrix[width + low : width + low + part_rows, first_slot * block :] - product
        sums.append(piece)
        outgoing = piece.reshape(
            part_rows // block // leaf_count, leaf_count, block, kept, block
        )
        received.append(
            lax.all_to_all(outgoing, "leaf", split_axis=1, concat_axis=1, tiled=True)
        )
    received = jnp.concatenate(received, 0)
    update = jnp.concatenate(sums, 0)

    all_leads = jnp.concatenate(lead_columns, 1)
    columns = []
    for slot in range(slots):
        pick = jnp.clip(slot * front_count + front_pos, 0, pivots - 1) * block
        if slot < panel_slots:
            pivot_column = jnp.concatenate(
                [
                    lax.dynamic_slice_in_dim(all_leads, pick, block, 1),
                    lax.dynamic_slice_in_dim(lower, pick, block, 1),
                ],
                0,
            )
        if slot < first_slot:
            columns.append(pivot_column)
            continue
        at = (slot - first_slot) * block
        column = jnp.concatenate(
            [jnp.zeros((width, block), jnp.float32), update[:, at : at + block]], 0
        )
        if slot < panel_slots:
            is_pivot = slot * front_count + front_pos < pivots
            column = jnp.where(is_pivot, pivot_column, column)
        columns.append(column)
    child_result = jnp.stack(columns, 1).reshape(child_fronts.shape)

    rslots = parent_front.shape[0]
    cslots = parent_front.shape[3]
    groups = child_map.shape[0]
    quota = update_count // leaf_count
    row_map = lax.dynamic_index_in_dim(
        child_map.reshape(groups, quota, leaf_count), leaf_pos, axis=2, keepdims=False
    )
    row_onehot = (
        (row_map // leaf_count)[:, :, None] == jnp.arange(rslots)[None, None, :]
    ).astype(jnp.float32)
    col_blocks = jnp.arange(first_slot, slots) * front_count + front_pos - pivots
    valid = col_blocks >= 0
    col_map = jnp.take(child_map, jnp.clip(col_blocks, 0, update_count - 1), axis=1)
    col_match = (col_map // front_count)[:, :, None] == jnp.arange(cslots)[None, None, :]
    col_onehot = (valid[None, :, None] & col_match).astype(jnp.float32)
    placed = jnp.einsum("gqa,qgxcy->gaxcy", row_onehot, received, precision=HIGH)
    summed = jnp.einsum("gcb,gaxcy->axby", col_onehot, placed, precision=HIGH)
    parent = parent_front.reshape(rslots * block, cslots * block)
    parent = parent + summed.reshape(rslots * block, cslots * block)

    count = PARENT_PIVOTS
    span = count * block
    row_panel = lax.all_gather(parent[:block], "leaf", axis=0)[:count]
    row_panel = row_panel.reshape(span, cslots * block)
    spread = lax.all_to_all(
        parent[:, :block].reshape(front_count, rslots * block // front_count, block),
        "front",
        split_axis=0,
        concat_axis=0,
        tiled=True,
    )[:count]
    spread = spread.transpose(1, 0, 2).reshape(rslots * block // front_count, span)
    col_panel = lax.all_gather(spread, "front", axis=0, tiled=True)
    square = lax.all_gather(col_panel[:block], "leaf", axis=0)[:count].reshape(span, span)
    work = jnp.concatenate([square, row_panel, col_panel.T], 1)
    strips = factor_strips(work, count, block)
    row_done = jnp.concatenate(
        [strip[:, (count - i) * block : (count - i + cslots) * block] for i, strip in enumerate(strips)], 0
    )
    col_done = jnp.concatenate(
        [strip[:, (count - i + cslots) * block :] for i, strip in enumerate(strips)], 0
    )
    factor = jnp.concatenate(
        [
            jnp.concatenate(
                [jnp.zeros((i * block, block), jnp.float32), strip[:, : span - i * block].T], 0
            )
            for i, strip in enumerate(strips)
        ],
        1,
    )
    columns_done = col_done.T
    product = lax.dot_general(
        columns_done, row_done, (((1,), (0,)), ((), ())), precision=HIGH
    )
    trailing = parent - product
    mine = jnp.clip(front_pos, 0, count - 1) * block
    pivot_column = lax.dynamic_slice_in_dim(columns_done, mine, block, 1)
    row_pick = jnp.clip(leaf_pos, 0, count - 1) * block
    head = lax.dynamic_slice(factor, (row_pick, mine), (block, block))
    row_is_pivot = leaf_pos < count
    col_is_pivot = front_pos < count
    pivot_column = jnp.concatenate(
        [jnp.where(row_is_pivot, head, pivot_column[:block]), pivot_column[block:]], 0
    )
    row_ids = jnp.arange(rslots * block)[:, None] < block
    trailing = jnp.where(row_is_pivot & row_ids, 0.0, trailing)
    first = jnp.where(col_is_pivot, pivot_column, trailing[:, :block])
    parent_result = jnp.concatenate([first, trailing[:, block:]], 1)
    return (child_result, parent_result.reshape(parent_front.shape))


def solution(mesh):
    return jax.shard_map(
        body,
        mesh=mesh,
        in_specs=(
            P("leaf", None, None, "front", None),
            P(None, "leaf", None, None, "front", None),
            P(),
        ),
        out_specs=(
            P("leaf", None, None, "front", None),
            P(None, "leaf", None, None, "front", None),
        ),
        check_vma=False,
    )
```

```python
import jax
import jax.numpy as jnp
from jax import lax
from jax.experimental import pallas as pl
from jax.experimental.pallas import tpu as pltpu
from jax.sharding import PartitionSpec as P

CHILD_PIVOTS = 8
PARENT_PIVOTS = 2
HIGH = lax.Precision.HIGH
HIGHEST = lax.Precision.HIGHEST


def strip_kernel(current_ref, strip_ref, square, inverse):
    n = current_ref.shape[0]
    width = current_ref.shape[1]
    square[...] = current_ref[:, :n]
    rows = lax.broadcasted_iota(jnp.int32, (n, n), 0)
    lanes = lax.broadcasted_iota(jnp.int32, (n, n), 1)
    inverse[...] = jnp.where(rows == lanes, 1.0, 0.0)
    slab_row = lax.broadcasted_iota(jnp.int32, (8, n), 0)
    slab_lane = lax.broadcasted_iota(jnp.int32, (8, n), 1)
    for low in range(0, n, 8):
        top = square[low : low + 8, :]
        ident = inverse[low : low + 8, :]
        wide = [
            jnp.broadcast_to(top[:, low + k : low + k + 1], (8, n)) for k in range(8)
        ]
        top = jnp.where(slab_lane >= low, top, 0.0)
        for k in range(8):
            pivot = wide[k][k : k + 1, :]
            root = lax.rsqrt(pivot)
            root = root * (1.5 - 0.5 * (pivot * root) * root)
            under = slab_row > k
            at = slab_row == k
            scale = jnp.where(under, wide[k] * root, 0.0)
            keep = jnp.where(at, root, 1.0)
            for m in range(k + 1, 8):
                wide[m] = wide[m] - scale * (wide[m][k : k + 1, :] * root)
            top = top * keep - scale * (top[k : k + 1, :] * root)
            ident = ident * keep - scale * (ident[k : k + 1, :] * root)
        top = jnp.where(slab_lane >= low + slab_row, top, 0.0)
        strip_ref[low : low + 8, :n] = top
        inverse[low : low + 8, :] = ident
        if low + 8 < n:
            both = jnp.concatenate([top, ident], 1)
            change = lax.dot_general(
                top, both, (((0,), (0,)), ((), ())),
                precision=HIGHEST, preferred_element_type=jnp.float32,
            )
            square[low + 8 :, :] = square[low + 8 :, :] - change[low + 8 :, :n]
            inverse[low + 8 :, :] = inverse[low + 8 :, :] - change[low + 8 :, n:]
    solver = inverse[...]
    for low in range(n, width, 2 * n):
        high = min(low + 2 * n, width)
        strip_ref[:, low:high] = jnp.dot(
            solver, current_ref[:, low:high],
            precision=HIGHEST, preferred_element_type=jnp.float32,
        )


def finish_strip(current):
    block, width = current.shape
    return pl.pallas_call(
        strip_kernel,
        out_shape=jax.ShapeDtypeStruct((block, width), jnp.float32),
        in_specs=[pl.BlockSpec(memory_space=pltpu.VMEM)],
        out_specs=pl.BlockSpec(memory_space=pltpu.VMEM),
        scratch_shapes=[
            pltpu.VMEM((block, block), jnp.float32),
            pltpu.VMEM((block, block), jnp.float32),
        ],
        compiler_params=pltpu.CompilerParams(vmem_limit_bytes=32 * 1024 * 1024),
        cost_estimate=pl.CostEstimate(
            flops=2 * block * block * (width + block),
            bytes_accessed=8 * block * width,
            transcendentals=block,
        ),
        name="strip",
    )(current)


def extend_kernel(row_ref, col_ref, *refs):
    parent_ref, out_ref = refs[-2], refs[-1]
    here = pl.program_id(0)
    block = parent_ref.shape[0]
    out_ref[...] = parent_ref[...]
    for group, child in enumerate(refs[:-2]):
        for slot in range(child.shape[3] // block):
            target = col_ref[group, slot]

            @pl.when((row_ref[group, here] >= 0) & (target >= 0))
            def _():
                span = pl.ds(pl.multiple_of(target * block, block), block)
                part = child[0, 0, :, slot * block : (slot + 1) * block]
                out_ref[:, span] = out_ref[:, span] + part


def extend_add(parent, received, row_index, col_index):
    groups, rslots = row_index.shape
    block = parent.shape[0] // rslots
    columns = parent.shape[1]
    wide = received.shape[3]

    def child_spec(group):
        return pl.BlockSpec(
            (1, 1, block, wide),
            lambda a, rows, cols: (jnp.maximum(rows[group, a], 0), group, 0, 0),
        )

    return pl.pallas_call(
        extend_kernel,
        out_shape=jax.ShapeDtypeStruct(parent.shape, jnp.float32),
        grid_spec=pltpu.PrefetchScalarGridSpec(
            num_scalar_prefetch=2,
            grid=(rslots,),
            in_specs=[child_spec(group) for group in range(groups)]
            + [pl.BlockSpec((block, columns), lambda a, rows, cols: (a, 0))],
            out_specs=pl.BlockSpec((block, columns), lambda a, rows, cols: (a, 0)),
        ),
        compiler_params=pltpu.CompilerParams(vmem_limit_bytes=32 * 1024 * 1024),
        cost_estimate=pl.CostEstimate(
            flops=parent.size, bytes_accessed=12 * parent.size, transcendentals=0
        ),
        name="extend_add",
    )(row_index, col_index, *([received] * groups), parent)


def factor_strips(work, pivots, block):
    strips = []
    for i in range(pivots):
        start = i * block
        current = work[start : start + block, start:]
        if strips:
            done = jnp.concatenate(
                [strip[:, (i - j) * block :] for j, strip in enumerate(strips)], 0
            )
            current = current - lax.dot_general(
                done[:, :block], done, (((0,), (0,)), ((), ())), precision=HIGHEST
            )
        strips.append(finish_strip(current))
    return strips


def body(child_fronts, parent_front, child_map):
    front_count = lax.axis_size("front")
    leaf_count = lax.axis_size("leaf")
    front_pos = lax.axis_index("front")
    leaf_pos = lax.axis_index("leaf")
    block = child_fronts.shape[4]
    order = child_fronts.shape[1]
    slots = child_fronts.shape[2]
    pivots = CHILD_PIVOTS
    width = pivots * block
    first_slot = pivots // front_count
    kept = slots - first_slot
    panel_slots = (pivots + front_count - 1) // front_count
    update_count = order // block - pivots
    matrix = child_fronts.reshape(order, slots * block)

    lead = matrix[:width, : panel_slots * block]
    if front_count == pivots:
        lead = jnp.broadcast_to(lead[None], (front_count,) + lead.shape)
        lead = lax.all_to_all(lead, "front", split_axis=0, concat_axis=0, tiled=True)
    else:
        lead = lax.all_gather(lead, "front", axis=0)
    lead = lead.reshape(front_count, width, panel_slots, block).transpose(1, 2, 0, 3)
    lead = lead.reshape(width, panel_slots * front_count * block)[:, :width]

    own_top = matrix[:width, first_slot * block :]
    strips = factor_strips(jnp.concatenate([lead, own_top], 1), pivots, block)
    gathered = []
    own = []
    lead_columns = []
    for i, strip in enumerate(strips):
        split = width - i * block
        own.append(strip[:, split:])
        column = strip[:, :split].T
        lead_columns.append(
            jnp.concatenate([jnp.zeros((i * block, block), jnp.float32), column], 0)
        )
    early = (3 * pivots) // 8
    for group in (own[:early], own[early:]):
        sent = jnp.concatenate(group, 0).T
        gathered.append(
            lax.all_gather(sent, "front", axis=0, tiled=True).reshape(
                front_count, kept, block, sent.shape[1]
            )
        )
    own = jnp.concatenate(own, 0)
    lower = jnp.concatenate(gathered, 3).transpose(1, 0, 2, 3)
    lower = lower.reshape(kept * front_count * block, width)
    lower = lower[width - first_slot * front_count * block :]

    parts = kept if update_count % (kept * leaf_count) == 0 else 1
    part_rows = update_count * block // parts
    sums = []
    received = []
    for part in range(parts):
        low = part * part_rows
        product = lax.dot_general(
            lower[low : low + part_rows], own, (((1,), (0,)), ((), ())), precision=HIGH
        )
        piece = matrix[width + low : width + low + part_rows, first_slot * block :] - product
        sums.append(piece)
        outgoing = piece.reshape(
            part_rows // block // leaf_count, leaf_count, block, kept * block
        )
        received.append(
            lax.all_to_all(outgoing, "leaf", split_axis=1, concat_axis=1, tiled=True)
        )
    received = jnp.concatenate(received, 0)
    update = jnp.concatenate(sums, 0)

    all_leads = jnp.concatenate(lead_columns, 1)
    columns = []
    for slot in range(slots):
        pick = jnp.clip(slot * front_count + front_pos, 0, pivots - 1) * block
        if slot < panel_slots:
            pivot_column = jnp.concatenate(
                [
                    lax.dynamic_slice_in_dim(all_leads, pick, block, 1),
                    lax.dynamic_slice_in_dim(lower, pick, block, 1),
                ],
                0,
            )
        if slot < first_slot:
            columns.append(pivot_column)
            continue
        at = (slot - first_slot) * block
        column = jnp.concatenate(
            [jnp.zeros((width, block), jnp.float32), update[:, at : at + block]], 0
        )
        if slot < panel_slots:
            is_pivot = slot * front_count + front_pos < pivots
            column = jnp.where(is_pivot, pivot_column, column)
        columns.append(column)
    child_result = jnp.stack(columns, 1).reshape(child_fronts.shape)

    rslots = parent_front.shape[0]
    cslots = parent_front.shape[3]
    groups = child_map.shape[0]
    quota = update_count // leaf_count
    row_map = lax.dynamic_index_in_dim(
        child_map.reshape(groups, quota, leaf_count), leaf_pos, axis=2, keepdims=False
    )
    hits = (row_map // leaf_count)[:, :, None] == jnp.arange(rslots)[None, None, :]
    steps = jnp.arange(quota, dtype=jnp.int32)[None, :, None]
    row_index = jnp.max(jnp.where(hits, steps, -1), axis=1)
    col_blocks = jnp.arange(first_slot, slots) * front_count + front_pos - pivots
    col_map = jnp.take(child_map, jnp.clip(col_blocks, 0, update_count - 1), axis=1)
    col_index = jnp.where((col_blocks >= 0)[None, :], col_map // front_count, -1)
    parent = extend_add(
        parent_front.reshape(rslots * block, cslots * block),
        received,
        row_index.astype(jnp.int32),
        col_index.astype(jnp.int32),
    )

    count = PARENT_PIVOTS
    span = count * block
    row_panel = lax.all_gather(parent[:block], "leaf", axis=0)[:count]
    row_panel = row_panel.reshape(span, cslots * block)
    spread = lax.all_to_all(
        parent[:, :block].reshape(front_count, rslots * block // front_count, block),
        "front",
        split_axis=0,
        concat_axis=0,
        tiled=True,
    )[:count]
    spread = spread.transpose(1, 0, 2).reshape(rslots * block // front_count, span)
    col_panel = lax.all_gather(spread, "front", axis=0, tiled=True)
    square = lax.all_gather(col_panel[:block], "leaf", axis=0)[:count].reshape(span, span)
    work = jnp.concatenate([square, row_panel, col_panel.T], 1)
    strips = factor_strips(work, count, block)
    row_done = jnp.concatenate(
        [strip[:, (count - i) * block : (count - i + cslots) * block] for i, strip in enumerate(strips)], 0
    )
    col_done = jnp.concatenate(
        [strip[:, (count - i + cslots) * block :] for i, strip in enumerate(strips)], 0
    )
    factor = jnp.concatenate(
        [
            jnp.concatenate(
                [jnp.zeros((i * block, block), jnp.float32), strip[:, : span - i * block].T], 0
            )
            for i, strip in enumerate(strips)
        ],
        1,
    )
    columns_done = col_done.T
    product = lax.dot_general(
        columns_done, row_done, (((1,), (0,)), ((), ())), precision=HIGH
    )
    trailing = parent - product
    mine = jnp.clip(front_pos, 0, count - 1) * block
    pivot_column = lax.dynamic_slice_in_dim(columns_done, mine, block, 1)
    row_pick = jnp.clip(leaf_pos, 0, count - 1) * block
    head = lax.dynamic_slice(factor, (row_pick, mine), (block, block))
    row_is_pivot = leaf_pos < count
    col_is_pivot = front_pos < count
    pivot_column = jnp.concatenate(
        [jnp.where(row_is_pivot, head, pivot_column[:block]), pivot_column[block:]], 0
    )
    row_ids = jnp.arange(rslots * block)[:, None] < block
    trailing = jnp.where(row_is_pivot & row_ids, 0.0, trailing)
    first = jnp.where(col_is_pivot, pivot_column, trailing[:, :block])
    parent_result = jnp.concatenate([first, trailing[:, block:]], 1)
    return (child_result, parent_result.reshape(parent_front.shape))


def solution(mesh):
    return jax.shard_map(
        body,
        mesh=mesh,
        in_specs=(
            P("leaf", None, None, "front", None),
            P(None, "leaf", None, None, "front", None),
            P(),
        ),
        out_specs=(
            P("leaf", None, None, "front", None),
            P(None, "leaf", None, None, "front", None),
        ),
        check_vma=False,
    )
```
